256 devices in a mesh: group: 16 (over z, x_hi), dp: 16 (over x_lo, y, core).
Axes of the slice: x: 4 (x_hi: 2, x_lo: 2; x = x_hi * 2 + x_lo), y: 4, z: 8, core: 2. Of those that a mesh axis runs over, the one named last changes fastest.
Arguments:
- img_feat: bfloat16 [16, 4096, 1152], P('group', 'dp'), may hold values from -6 to 6
- txt_feat: bfloat16 [16, 4096, 1152], P('group', 'dp'), may hold values from -6 to 6
- group_weights: bfloat16 [16, 2, 1152, 1152], P('group', None, 'dp'), may hold values from -0.1875 to 0.1875
- drift: bfloat16 [16, 2, 1152, 1152], P('group', None, 'dp'), may hold values from -3 to 3
- logit_params: float32 [2], replicated, may hold values from -2 to 3, as said below
Outputs:
- outer_step: float32 [2, 1152, 1152], P(None, 'dp')
The draws below stay inside these ranges and needn't reach their ends.
Inputs may be any that keep to these rules, and one draw needn't show every extreme that they name: logit_params[0] lies in 2 to 3 and logit_params[1] in -2 to 0.
All inputs are finite; a program needn't handle non-finite values.
Results may differ from the reference program's by a relative error of at most 0.012.
Values may be sent and summed in bfloat16 or wider, within the bound.
No kernel may reach another device: no remote copies, remote signals or barrier semaphores. Data moves between devices by JAX's collectives and lax.ppermute only.
A program may use at most 128 MiB of HBM per device.

```python
import jax
import jax.numpy as jnp
from jax import lax

D = 1152
E = 1152
TOK_DEV = 256
BATCH = 4096
GROUPS = 16
N_DP = 16


def draw_logit_params(key, part):
    key = jax.random.fold_in(key, 7)
    first = jax.random.uniform(jax.random.fold_in(key, 1), (1,), jnp.float32, 2.0, 3.0)
    second = jax.random.uniform(jax.random.fold_in(key, 2), (1,), jnp.float32, -2.0, 0.0)
    return jnp.concatenate([first, second])


def steps_of(stream_key, shape, shards, low, largest):
    factor_of, own = 1.0, jax.random.fold_in(stream_key, 6)
    for position, shards_of in shards:
        heights = jnp.exp(jax.random.uniform(jax.random.fold_in(own, position), (shards_of,), jnp.float32, low / len(shards), largest / len(shards)))
        factor_of = factor_of * jnp.repeat(heights, shape[position] // shards_of).reshape([-1 if axis == position else 1 for axis in range(len(shape))])
    return factor_of


def gaussian(key, shape, scale, reach, shards=(), kind=jnp.bfloat16):
    array = scale * jax.random.normal(key, shape, jnp.float32)
    if shards:
        array = array * steps_of(key, shape, shards, -0.22, 0.18)
    return jnp.clip(array, -reach, reach).astype(kind)


def setup_inputs(seed: int = 0) -> dict:
    key_list = jax.random.split(jax.random.key(seed), 6)
    img_feat = gaussian(key_list[0], (GROUPS, BATCH, D), 1.0, 6.0, ((0, 16), (1, 16)))
    txt_feat = gaussian(key_list[1], (GROUPS, BATCH, D), 1.0, 6.0, ((0, 16), (1, 16)))
    group_weights = gaussian(key_list[2], (GROUPS, 2, D, E), D ** -0.5, 0.1875, ((0, 16), (2, 16)))
    drift = gaussian(key_list[3], (GROUPS, 2, D, E), 0.5, 3.0, ((0, 16), (2, 16)))
    logit_params = draw_logit_params(jax.random.fold_in(key_list[5], 71), 0)
    return {"img_feat": img_feat, "txt_feat": txt_feat, "group_weights": group_weights, "drift": drift, "logit_params": logit_params}


def embed(feats, weight):
    raw = jnp.dot(feats, weight, preferred_element_type=jnp.float32)
    nrm = jnp.sqrt(lax.optimization_barrier(jnp.sum(raw * raw, axis=1, keepdims=True)) + 1e-06)
    return (raw / nrm, nrm)

def back_norm(unit, nrm, dz):
    return ((dz - unit * lax.optimization_barrier(jnp.sum(unit * dz, axis=1, keepdims=True))) / nrm).astype(jnp.bfloat16)

def reference(img_feat, txt_feat, group_weights, drift, logit_params):
    scale = jnp.exp(logit_params[0])
    bias = logit_params[1]

    def one_group(inputs):
        x_img, x_txt, weights, shift = inputs
        zf_img, n_img = embed(x_img, weights[0])
        zf_txt, n_txt = embed(x_txt, weights[1])
        z_img = zf_img.astype(jnp.bfloat16)
        z_txt = zf_txt.astype(jnp.bfloat16)
        s = scale * jnp.dot(z_img, z_txt.T, preferred_element_type=jnp.float32) + bias
        label = jnp.where(jnp.eye(BATCH, dtype=jnp.bool_), 1.0, -1.0).astype(jnp.float32)
        gb = (-label * jax.nn.sigmoid(-label * s)).astype(jnp.bfloat16)
        dz_img = scale * jnp.dot(gb, z_txt, preferred_element_type=jnp.float32)
        gk = gb.reshape(N_DP, TOK_DEV, BATCH).astype(jnp.float32)
        zk = z_img.reshape(N_DP, TOK_DEV, E).astype(jnp.float32)
        parts = (scale * jnp.einsum('kij,kie->kje', gk, zk)).astype(jnp.bfloat16)
        parts = lax.optimization_barrier(parts)
        dz_txt = lax.optimization_barrier(jnp.sum(parts.astype(jnp.float32), axis=0))
        du_img = back_norm(zf_img, n_img, dz_img)
        du_txt = back_norm(zf_txt, n_txt, dz_txt)
        grad_img = jnp.dot(x_img.T, du_img, preferred_element_type=jnp.float32)
        grad_txt = jnp.dot(x_txt.T, du_txt, preferred_element_type=jnp.float32)
        return shift.astype(jnp.float32) + jnp.stack([grad_img, grad_txt])
    pseudo = lax.map(one_group, (img_feat, txt_feat, group_weights, drift))
    return lax.optimization_barrier(jnp.sum(pseudo, axis=0)) / GROUPS
```

```python
import jax
import jax.numpy as jnp
from jax import lax
from jax.sharding import Mesh, PartitionSpec as P

BF = jnp.bfloat16
F32 = jnp.float32
CHIPS = ("xl", "y")
GROUP = ("z", "xh")


def shift_y(x, by):
    return lax.ppermute(x, "y", [(i, (i + by) % 4) for i in range(4)])


def swap_x(x):
    return lax.ppermute(x, "xl", [(0, 1), (1, 0)])


def swap_core(x):
    return lax.ppermute(x, "c", [(0, 1), (1, 0)])


def exchange(x, axes):
    return lax.all_to_all(x, axes, split_axis=0, concat_axis=0, tiled=True)


def dot(a, b, dims):
    return lax.dot_general(a, b, (dims, ((), ())), preferred_element_type=F32)


def embed(x, w):
    u = dot(x, w, ((1,), (0,)))
    nrm = jnp.sqrt(jnp.sum(u * u, axis=1, keepdims=True) + 1e-06)
    return u / nrm, nrm


def back_norm(unit, nrm, dz):
    return ((dz - unit * jnp.sum(unit * dz, axis=1, keepdims=True)) / nrm).astype(BF)


def local(img_feat, txt_feat, group_weights, drift, logit_params):
    core = lax.axis_index("c")
    first = core == 0
    x_img, x_txt = img_feat[0], txt_feat[0]
    rows = x_img.shape[0]
    scale = jnp.exp(logit_params[0])
    bias = logit_params[1]

    weights = lax.all_gather(group_weights[0], ("xl", "y", "c"), axis=1, tiled=True)
    txt_x = swap_x(x_txt)
    x_img = jnp.concatenate([x_img, shift_y(x_img, 1), shift_y(x_img, 3), shift_y(x_img, 2)], 0)
    x_txt = jnp.concatenate([x_txt, swap_core(x_txt), txt_x, swap_core(txt_x)], 0)
    kept, given = jnp.where(first, drift[0, 0], drift[0, 1]), jnp.where(first, drift[0, 1], drift[0, 0])
    got = swap_core(given)
    shift = jnp.concatenate([jnp.where(first, kept, got), jnp.where(first, got, kept)], 0)

    zf_img, n_img = embed(x_img, weights[0])
    zf_txt, n_txt = embed(x_txt, weights[1])
    z_img, z_txt = zf_img.astype(BF), zf_txt.astype(BF)
    score = scale * dot(z_img, z_txt, ((1,), (1,))) + bias
    i = lax.broadcasted_iota(jnp.int32, score.shape, 0)
    j = lax.broadcasted_iota(jnp.int32, score.shape, 1)
    label = jnp.where((i == j) & (i < rows), 1.0, -1.0).astype(F32)
    gb = (-label * jax.nn.sigmoid(-label * score)).astype(BF)
    du_img = back_norm(zf_img, n_img, scale * dot(gb, z_txt, ((1,), (0,))))
    du_txt = back_norm(zf_txt, n_txt, scale * dot(gb, z_img, ((0,), (0,))))
    g_img = dot(x_img, du_img, ((0,), (0,))).astype(BF)
    g_txt = dot(x_txt, du_txt, ((0,), (0,))).astype(BF)

    mine = jnp.where(first, g_img, g_txt).astype(F32) + swap_core(jnp.where(first, g_txt, g_img)).astype(F32)
    d, e = mine.shape
    parts = exchange(mine.astype(BF).reshape(8, d // 8, e), CHIPS)
    block = jnp.sum(parts.astype(F32), axis=0) + shift.astype(F32)
    h = d // 8
    tiles = block.reshape(h // 8, 8, e // 128, 128).transpose(0, 2, 1, 3).reshape(-1, 8, 128)
    n = tiles.shape[0]
    each = -(-n // 16)
    tiles = jnp.pad(tiles, ((0, 16 * each - n), (0, 0), (0, 0))).reshape(16, each * 8, 128)
    total = jnp.sum(exchange(tiles.astype(BF), GROUP).astype(F32), axis=0) * (1.0 / 16)
    out = exchange(jnp.broadcast_to(total[None], (16, each * 8, 128)), GROUP)
    out = out.reshape(16 * each, 8, 128)[:n].reshape(h // 8, e // 128, 8, 128).transpose(0, 2, 1, 3)
    out = out.reshape(2, h // 2, e)
    keep = jnp.where(first, out[0], out[1])
    other = swap_core(jnp.where(first, out[1], out[0]))
    return jnp.stack([jnp.where(first, keep, other), jnp.where(first, other, keep)])


def solution(mesh):
    fine = Mesh(mesh.devices.reshape(8, 2, 2, 4, 2), ("z", "xh", "xl", "y", "c"))
    dp = ("xl", "y", "c")
    return jax.shard_map(
        local,
        mesh=fine,
        in_specs=(
            P(GROUP, dp, None),
            P(GROUP, dp, None),
            P(GROUP, None, dp, None),
            P(GROUP, None, dp, None),
            P(),
        ),
        out_specs=P(None, dp, None),
        check_vma=False,
    )
```

```python
import jax
import jax.numpy as jnp
from jax import lax
from jax.sharding import Mesh, PartitionSpec as P

BF = jnp.bfloat16
F32 = jnp.float32
CHIPS = ("xl", "y")
GROUP = ("z", "xh")


def shift_y(x, by):
    return lax.ppermute(x, "y", [(i, (i + by) % 4) for i in range(4)])


def swap_x(x):
    return lax.ppermute(x, "xl", [(0, 1), (1, 0)])


def swap_core(x):
    return lax.ppermute(x, "c", [(0, 1), (1, 0)])


def exchange(x, axes):
    return lax.all_to_all(x, axes, split_axis=0, concat_axis=0, tiled=True)


def dot(a, b, dims):
    return lax.dot_general(a, b, (dims, ((), ())), preferred_element_type=F32)


def embed(x, w):
    u = dot(x, w, ((1,), (0,)))
    nrm = jnp.sqrt(jnp.sum(u * u, axis=1, keepdims=True) + 1e-06)
    return u / nrm, nrm


def back_norm(unit, nrm, dz):
    return ((dz - unit * jnp.sum(unit * dz, axis=1, keepdims=True)) / nrm).astype(BF)


def local(img_feat, txt_feat, group_weights, drift, logit_params):
    core = lax.axis_index("c")
    x_img, x_txt = img_feat[0], txt_feat[0]
    rows = x_img.shape[0]
    scale = jnp.exp(logit_params[0])
    bias = logit_params[1]

    weights = lax.all_gather(group_weights[0], ("xl", "y", "c"), axis=1, tiled=True)
    txt_x = swap_x(x_txt)
    below, above = shift_y(x_img, 1), shift_y(x_img, 3)
    half = rows // 2
    x_img = jnp.concatenate([x_img, below, above, shift_y(below[:half], 1), shift_y(above[half:], 3)], 0)
    x_txt = jnp.concatenate([x_txt, swap_core(x_txt), txt_x, swap_core(txt_x)], 0)

    def columns(x):
        parts = x.T.reshape(8, 2, -1, x.shape[0])
        pick = lambda k: lax.dynamic_index_in_dim(parts, k, 1, keepdims=False).reshape(-1, x.shape[0])
        return pick(core), pick(1 - core)

    keep_img, give_img = columns(x_img)
    keep_txt, give_txt = columns(x_txt)

    zf_txt, n_txt = embed(x_txt, weights[1])
    zf_img, n_img = embed(x_img, weights[0])
    z_img, z_txt = zf_img.astype(BF), zf_txt.astype(BF)
    score = scale * dot(z_img, z_txt, ((1,), (1,))) + bias
    i = lax.broadcasted_iota(jnp.int32, score.shape, 0)
    j = lax.broadcasted_iota(jnp.int32, score.shape, 1)
    label = jnp.where((i == j) & (i < rows), 1.0, -1.0).astype(F32)
    gb = (-label * jax.nn.sigmoid(-label * score)).astype(BF)
    nn = ((1,), (0,))
    du_txt = back_norm(zf_txt, n_txt, scale * dot(gb, z_img, ((0,), (0,))))
    got_txt = swap_core(dot(give_txt, du_txt, nn).astype(BF))
    du_img = back_norm(zf_img, n_img, scale * dot(gb, z_txt, nn))
    got_img = swap_core(dot(give_img, du_img, nn).astype(BF))
    g_txt = dot(keep_txt, du_txt, nn)
    g_img = dot(keep_img, du_img, nn)
    d, e = g_img.shape
    h = d // 8
    sums = [(g + got.astype(F32)).astype(BF).reshape(8, h, e) for g, got in ((g_img, got_img), (g_txt, got_txt))]
    parts = exchange(jnp.stack(sums, 1), CHIPS)
    block = jnp.sum(parts.astype(F32), axis=0) + drift[0].astype(F32)
    tiles = block.reshape(2 * h // 8, 8, e // 128, 128).transpose(0, 2, 1, 3).reshape(-1, 8, 128)
    n = tiles.shape[0]
    each = -(-n // 16)
    tiles = jnp.pad(tiles, ((0, 16 * each - n), (0, 0), (0, 0))).reshape(16, each * 8, 128)
    total = jnp.sum(exchange(tiles.astype(BF), GROUP).astype(F32), axis=0) * (1.0 / 16)
    out = exchange(jnp.broadcast_to(total.astype(BF)[None], (16, each * 8, 128)), GROUP).astype(F32)
    out = out.reshape(16 * each, 8, 128)[:n].reshape(2 * h // 8, e // 128, 8, 128).transpose(0, 2, 1, 3)
    return out.reshape(2, h, e)


def solution(mesh):
    fine = Mesh(mesh.devices.reshape(8, 2, 2, 4, 2), ("z", "xh", "xl", "y", "c"))
    dp = ("xl", "y", "c")
    return jax.shard_map(
        local,
        mesh=fine,
        in_specs=(
            P(GROUP, dp, None),
            P(GROUP, dp, None),
            P(GROUP, None, dp, None),
            P(GROUP, None, dp, None),
            P(),
        ),
        out_specs=P(None, dp, None),
        check_vma=False,
    )
```

```python
import jax
import jax.numpy as jnp
from jax import lax
from jax.sharding import Mesh, PartitionSpec as P

BF = jnp.bfloat16
F32 = jnp.float32
CHIPS = ("xl", "y")
GROUP = ("z", "xh")


def shift_y(x, by):
    return lax.ppermute(x, "y", [(i, (i + by) % 4) for i in range(4)])


def swap_x(x):
    return lax.ppermute(x, "xl", [(0, 1), (1, 0)])


def swap_core(x):
    return lax.ppermute(x, "c", [(0, 1), (1, 0)])


def exchange(x, axes):
    return lax.all_to_all(x, axes, split_axis=0, concat_axis=0, tiled=True)


def dot(a, b, dims):
    return lax.dot_general(a, b, (dims, ((), ())), preferred_element_type=F32)


def embed(x, w):
    u = dot(x, w, ((1,), (0,)))
    nrm = jnp.sqrt(jnp.sum(u * u, axis=1, keepdims=True) + 1e-06)
    return u / nrm, nrm


def back_norm(unit, nrm, dz):
    return ((dz - unit * jnp.sum(unit * dz, axis=1, keepdims=True)) / nrm).astype(BF)


def gather_ring(w):
    pair = jnp.stack([w, swap_x(w)])
    below, above = shift_y(pair, 1), shift_y(pair, 3)
    far = jnp.stack([shift_y(below[0], 1), shift_y(above[1], 3)])
    held = jnp.stack([pair, above, far, below])
    both = jnp.stack([held, swap_core(held)], 2)
    y, xl, core = (lax.axis_index(name) for name in ("y", "xl", "c"))
    both = lax.dynamic_slice_in_dim(jnp.concatenate([both, both], 0), lax.rem(4 - y, 4), 4, 0)
    both = jnp.where(xl == 0, both, both[:, ::-1])
    both = jnp.where(core == 0, both, both[:, :, ::-1])
    return both.transpose(1, 0, 2, 3, 4).reshape(-1, w.shape[1])


def local(img_feat, txt_feat, group_weights, drift, logit_params):
    core = lax.axis_index("c")
    x_img, x_txt = img_feat[0], txt_feat[0]
    rows = x_img.shape[0]
    scale = jnp.exp(logit_params[0])
    bias = logit_params[1]

    w_img = lax.all_gather(group_weights[0, 0], ("xl", "y", "c"), axis=0, tiled=True)
    w_txt = gather_ring(group_weights[0, 1])
    txt_x = swap_x(x_txt)
    below, above = shift_y(x_img, 1), shift_y(x_img, 3)
    half = rows // 2
    x_img = jnp.concatenate([x_img, below, above, shift_y(below[:half], 1), shift_y(above[half:], 3)], 0)
    x_txt = jnp.concatenate([x_txt, swap_core(x_txt), txt_x, swap_core(txt_x)], 0)

    def columns(x):
        parts = x.T.reshape(8, 2, -1, x.shape[0])
        pick = lambda k: lax.dynamic_index_in_dim(parts, k, 1, keepdims=False).reshape(-1, x.shape[0])
        return pick(core), pick(1 - core)

    keep_img, give_img = columns(x_img)
    keep_txt, give_txt = columns(x_txt)

    zf_txt, n_txt = embed(x_txt, w_txt)
    zf_img, n_img = embed(x_img, w_img)
    z_img, z_txt = zf_img.astype(BF), zf_txt.astype(BF)
    score = scale * dot(z_img, z_txt, ((1,), (1,))) + bias
    i = lax.broadcasted_iota(jnp.int32, score.shape, 0)
    j = lax.broadcasted_iota(jnp.int32, score.shape, 1)
    label = jnp.where((i == j) & (i < rows), 1.0, -1.0).astype(F32)
    gb = (-label * jax.nn.sigmoid(-label * score)).astype(BF)
    nn = ((1,), (0,))
    du_txt = back_norm(zf_txt, n_txt, scale * dot(gb, z_img, ((0,), (0,))))
    got_txt = swap_core(dot(give_txt, du_txt, nn).astype(BF))
    du_img = back_norm(zf_img, n_img, scale * dot(gb, z_txt, nn))
    got_img = swap_core(dot(give_img, du_img, nn).astype(BF))
    g_txt = dot(keep_txt, du_txt, nn)
    g_img = dot(keep_img, du_img, nn)
    d, e = g_img.shape
    h = d // 8
    sums = [(g + got.astype(F32)).astype(BF).reshape(8, h, e) for g, got in ((g_img, got_img), (g_txt, got_txt))]
    parts = exchange(jnp.stack(sums, 1), CHIPS)
    block = jnp.sum(parts.astype(F32), axis=0) + drift[0].astype(F32)
    tiles = block.reshape(2 * h // 8, 8, e // 128, 128).transpose(0, 2, 1, 3).reshape(-1, 8, 128)
    n = tiles.shape[0]
    each = -(-n // 16)
    tiles = jnp.pad(tiles, ((0, 16 * each - n), (0, 0), (0, 0))).reshape(16, each * 8, 128)
    total = jnp.sum(exchange(tiles.astype(BF), GROUP).astype(F32), axis=0) * (1.0 / 16)
    out = exchange(jnp.broadcast_to(total.astype(BF)[None], (16, each * 8, 128)), GROUP).astype(F32)
    out = out.reshape(16 * each, 8, 128)[:n].reshape(2 * h // 8, e // 128, 8, 128).transpose(0, 2, 1, 3)
    return out.reshape(2, h, e)


def solution(mesh):
    fine = Mesh(mesh.devices.reshape(8, 2, 2, 4, 2), ("z", "xh", "xl", "y", "c"))
    dp = ("xl", "y", "c")
    return jax.shard_map(
        local,
        mesh=fine,
        in_specs=(
            P(GROUP, dp, None),
            P(GROUP, dp, None),
            P(GROUP, None, dp, None),
            P(GROUP, None, dp, None),
            P(),
        ),
        out_specs=P(None, dp, None),
        check_vma=False,
    )
```

```python
import jax
import jax.numpy as jnp
from jax import lax
from jax.sharding import Mesh, PartitionSpec as P

BF = jnp.bfloat16
F32 = jnp.float32
CHIPS = ("xl", "y")
GROUP = ("z", "xh")


def shift_y(x, by):
    return lax.ppermute(x, "y", [(i, (i + by) % 4) for i in range(4)])


def swap_x(x):
    return lax.ppermute(x, "xl", [(0, 1), (1, 0)])


def swap_core(x):
    return lax.ppermute(x, "c", [(0, 1), (1, 0)])


def exchange(x, axes):
    return lax.all_to_all(x, axes, split_axis=0, concat_axis=0, tiled=True)


def dot(a, b, dims):
    return lax.dot_general(a, b, (dims, ((), ())), preferred_element_type=F32)


def embed(x, w):
    u = dot(x, w, ((1,), (0,)))
    nrm = jnp.sqrt(jnp.sum(u * u, axis=1, keepdims=True) + 1e-06)
    return u / nrm, nrm


def back_norm(unit, nrm, dz):
    return ((dz - unit * jnp.sum(unit * dz, axis=1, keepdims=True)) / nrm).astype(BF)


def local(img_feat, txt_feat, group_weights, drift, logit_params):
    core = lax.axis_index("c")
    x_img, x_txt = img_feat[0], txt_feat[0]
    rows = x_img.shape[0]
    scale = jnp.exp(logit_params[0])
    bias = logit_params[1]

    weights = lax.all_gather(group_weights[0], ("xl", "y", "c"), axis=1, tiled=True)
    txt_x = swap_x(x_txt)
    below, above = shift_y(x_img, 1), shift_y(x_img, 3)
    half = rows // 2
    x_img = jnp.concatenate([x_img, below, above, shift_y(below[:half], 1), shift_y(above[half:], 3)], 0)
    x_half = jnp.concatenate([x_txt, txt_x], 0)
    x_txt = jnp.concatenate([x_half, swap_core(x_half)], 0)

    xl, y = lax.axis_index("xl"), lax.axis_index("y")
    at = lambda v, k, axis: lax.dynamic_index_in_dim(v, k, axis, keepdims=False)

    def columns(x):
        parts = x.T.reshape(2, 4, 2, -1, x.shape[0])
        parts = jnp.concatenate([parts, parts], 1)
        parts = lax.dynamic_slice_in_dim(parts, y, 4, 1)
        parts = jnp.stack([at(parts, xl, 0), at(parts, 1 - xl, 0)])
        pick = lambda k: at(parts, k, 2).reshape(-1, x.shape[0])
        return pick(core), pick(1 - core)

    keep_img, give_img = columns(x_img)
    keep_txt, _ = columns(x_txt)

    zf_half, n_half = embed(x_half, weights[1])
    z_half = zf_half.astype(BF)
    z_txt = jnp.concatenate([z_half, swap_core(z_half)], 0)
    n_txt = jnp.concatenate([n_half, swap_core(n_half)], 0)
    zf_img, n_img = embed(x_img, weights[0])
    z_img = zf_img.astype(BF)
    score = scale * dot(z_img, z_txt, ((1,), (1,))) + bias
    i = lax.broadcasted_iota(jnp.int32, score.shape, 0)
    j = lax.broadcasted_iota(jnp.int32, score.shape, 1)
    label = jnp.where((i == j) & (i < rows), 1.0, -1.0).astype(F32)
    gb = (-label * jax.nn.sigmoid(-label * score)).astype(BF)
    nn = ((1,), (0,))
    du_txt = back_norm(z_txt.astype(F32), n_txt, scale * dot(gb, z_img, ((0,), (0,))))
    got_txt = swap_core(jnp.concatenate([du_txt[2 * rows :], du_txt[: 2 * rows]], 0))
    du_img = back_norm(zf_img, n_img, scale * dot(gb, z_txt, nn))
    got_img = swap_core(dot(give_img, du_img, nn).astype(BF))
    g_txt = dot(keep_txt, (du_txt.astype(F32) + got_txt.astype(F32)).astype(BF), nn).astype(BF)
    g_txt, got_img = lax.optimization_barrier((g_txt, got_img))
    g_img = dot(keep_img, du_img, nn)
    d, e = g_img.shape
    h = d // 8
    g_txt = g_txt.reshape(2, 4, h, e)
    g_img = (g_img + got_img.astype(F32)).astype(BF).reshape(2, 4, h, e)
    g_txt = (g_txt[0].astype(F32) + swap_x(g_txt[1]).astype(F32)).astype(BF)
    g_img = sum([g_img[:, 0].astype(F32)] + [shift_y(g_img[:, k], k).astype(F32) for k in (1, 2, 3)]).astype(BF)
    g_img = g_img[0].astype(F32) + swap_x(g_img[1]).astype(F32)
    g_txt = sum([g_txt[0].astype(F32)] + [shift_y(g_txt[k], k).astype(F32) for k in (1, 2, 3)])
    block = jnp.stack([g_img, g_txt]) + drift[0].astype(F32)
    tiles = block.reshape(2 * h // 8, 8, e // 128, 128).transpose(0, 2, 1, 3).reshape(-1, 8, 128)
    n = tiles.shape[0]
    each = -(-n // 16)
    tiles = jnp.pad(tiles, ((0, 16 * each - n), (0, 0), (0, 0))).reshape(16, each * 8, 128)
    total = jnp.sum(exchange(tiles.astype(BF), GROUP).astype(F32), axis=0) * (1.0 / 16)
    out = exchange(jnp.broadcast_to(total.astype(BF)[None], (16, each * 8, 128)), GROUP).astype(F32)
    out = out.reshape(16 * each, 8, 128)[:n].reshape(2 * h // 8, e // 128, 8, 128).transpose(0, 2, 1, 3)
    return out.reshape(2, h, e)


def solution(mesh):
    fine = Mesh(mesh.devices.reshape(8, 2, 2, 4, 2), ("z", "xh", "xl", "y", "c"))
    dp = ("xl", "y", "c")
    return jax.shard_map(
        local,
        mesh=fine,
        in_specs=(
            P(GROUP, dp, None),
            P(GROUP, dp, None),
            P(GROUP, None, dp, None),
            P(GROUP, None, dp, None),
            P(),
        ),
        out_specs=P(None, dp, None),
        check_vma=False,
    )
```

```python
import jax
import jax.numpy as jnp
from jax import lax
from jax.sharding import Mesh, PartitionSpec as P

BF = jnp.bfloat16
F32 = jnp.float32
CHIPS = ("xl", "y")
GROUP = ("z", "xh")


def shift_y(x, by):
    return lax.ppermute(x, "y", [(i, (i + by) % 4) for i in range(4)])


def swap_x(x):
    return lax.ppermute(x, "xl", [(0, 1), (1, 0)])


def swap_core(x):
    return lax.ppermute(x, "c", [(0, 1), (1, 0)])


def exchange(x, axes):
    return lax.all_to_all(x, axes, split_axis=0, concat_axis=0, tiled=True)


def dot(a, b, dims):
    return lax.dot_general(a, b, (dims, ((), ())), preferred_element_type=F32)


def embed(x, w):
    u = dot(x, w, ((1,), (0,)))
    nrm = jnp.sqrt(jnp.sum(u * u, axis=1, keepdims=True) + 1e-06)
    return u / nrm, nrm


def back_norm(unit, nrm, dz):
    return ((dz - unit * jnp.sum(unit * dz, axis=1, keepdims=True)) / nrm).astype(BF)


def after(x, *done):
    return lax.optimization_barrier((x, *done))[0]


def natural(held):
    both = jnp.stack([held, swap_core(held)], 2)
    y, xl, core = (lax.axis_index(name) for name in ("y", "xl", "c"))
    both = lax.dynamic_slice_in_dim(jnp.concatenate([both, both], 0), lax.rem(4 - y, 4), 4, 0)
    both = jnp.where(xl == 0, both, both[:, ::-1])
    both = jnp.where(core == 0, both, both[:, :, ::-1])
    return both.transpose(1, 0, 2, 3, 4).reshape(-1, held.shape[-1])


def gather_inputs(a, b, x_img, x_txt):
    cut = 40
    other = swap_x(a)
    pair = jnp.stack([a, other])
    below, above = shift_y(b, 1), shift_y(b, 3)
    a_below, a_above = shift_y(pair, 1), shift_y(pair, 3)
    near = jnp.stack([b, above, below])
    near_x = swap_x(near)
    far = jnp.concatenate([shift_y(below[:cut], 1), shift_y(above[cut:], 3)], 0)
    a_far = jnp.stack([shift_y(a_below[0], 1), shift_y(a_above[1], 3)])
    far_x = swap_x(far)
    held = [jnp.stack([near[0], near_x[0]]), jnp.stack([near[1], near_x[1]]), jnp.stack([far, far_x]), jnp.stack([near[2], near_x[2]])]
    w_b = natural(jnp.stack(held))
    w_a = natural(jnp.stack([pair, a_above, a_far, a_below]))
    x_img, x_txt = after(x_img, a_below, a_above), after(x_txt, near_x)
    return w_a, w_b, x_img, x_txt


def local(img_feat, txt_feat, group_weights, drift, logit_params):
    core = lax.axis_index("c")
    x_img, x_txt = img_feat[0], txt_feat[0]
    rows = x_img.shape[0]
    scale = jnp.exp(logit_params[0])
    bias = logit_params[1]

    w_img, w_txt, x_img, x_late = gather_inputs(group_weights[0, 0], group_weights[0, 1], x_img, x_txt)
    txt_x = swap_x(x_late)
    below, above = shift_y(x_img, 1), shift_y(x_img, 3)
    half = rows // 2
    far = shift_y(below[:half], 1), shift_y(above[half:], 3)
    x_half = jnp.concatenate([x_txt, txt_x], 0)
    x_txt = jnp.concatenate([x_half, swap_core(x_half)], 0)
    w_txt, x_txt = lax.optimization_barrier((w_txt, x_txt))
    zf_txt, n_txt = embed(x_txt, w_txt)
    *far, w_img = lax.optimization_barrier((*far, w_img, n_txt))[:3]
    x_img = jnp.concatenate([x_img, below, above, *far], 0)

    xl, y = lax.axis_index("xl"), lax.axis_index("y")
    at = lambda v, k, axis: lax.dynamic_index_in_dim(v, k, axis, keepdims=False)

    def columns(x):
        parts = x.T.reshape(2, 4, 2, -1, x.shape[0])
        parts = jnp.concatenate([parts, parts], 1)
        parts = lax.dynamic_slice_in_dim(parts, y, 4, 1)
        parts = jnp.stack([at(parts, xl, 0), at(parts, 1 - xl, 0)])
        pick = lambda k: at(parts, k, 2).reshape(-1, x.shape[0])
        return pick(core), pick(1 - core)

    keep_img, give_img = columns(x_img)
    keep_txt, _ = columns(x_txt)

    zf_img, n_img = embed(x_img, w_img)
    z_img, z_txt = zf_img.astype(BF), zf_txt.astype(BF)
    score = scale * dot(z_img, z_txt, ((1,), (1,))) + bias
    i = lax.broadcasted_iota(jnp.int32, score.shape, 0)
    j = lax.broadcasted_iota(jnp.int32, score.shape, 1)
    label = jnp.where((i == j) & (i < rows), 1.0, -1.0).astype(F32)
    gb = (-label * jax.nn.sigmoid(-label * score)).astype(BF)
    nn = ((1,), (0,))
    du_txt = back_norm(zf_txt, n_txt, scale * dot(gb, z_img, ((0,), (0,))))
    got_txt = swap_core(jnp.concatenate([du_txt[2 * rows :], du_txt[: 2 * rows]], 0))
    du_img = back_norm(zf_img, n_img, scale * dot(gb, z_txt, nn))
    got_img = swap_core(dot(give_img, du_img, nn).astype(BF))
    g_txt = dot(keep_txt, (du_txt.astype(F32) + got_txt.astype(F32)).astype(BF), nn).astype(BF)
    g_txt, got_img = lax.optimization_barrier((g_txt, got_img))
    g_img = dot(keep_img, du_img, nn)
    d, e = g_img.shape
    h = d // 8
    g_txt = g_txt.reshape(2, 4, h, e)
    g_img = (g_img + got_img.astype(F32)).astype(BF).reshape(2, 4, h, e)
    sums = lambda v: sum([v[0].astype(F32)] + [shift_y(v[k], k).astype(F32) for k in (1, 2, 3)])
    g_txt = sums(jnp.moveaxis(g_txt, 1, 0)).astype(BF)
    g_img = (g_img[0].astype(F32) + swap_x(g_img[1]).astype(F32)).astype(BF)
    g_txt = g_txt[0].astype(F32) + swap_x(g_txt[1]).astype(F32)
    g_img = sums(g_img)
    block = jnp.stack([g_img, g_txt]) + drift[0].astype(F32)
    tiles = block.reshape(2 * h // 8, 8, e // 128, 128).transpose(0, 2, 1, 3).reshape(-1, 8, 128)
    n = tiles.shape[0]
    each = -(-n // 16)
    tiles = jnp.pad(tiles, ((0, 16 * each - n), (0, 0), (0, 0))).reshape(16, each * 8, 128)
    total = jnp.sum(exchange(tiles.astype(BF), GROUP).astype(F32), axis=0) * (1.0 / 16)
    out = exchange(jnp.broadcast_to(total.astype(BF)[None], (16, each * 8, 128)), GROUP).astype(F32)
    out = out.reshape(16 * each, 8, 128)[:n].reshape(2 * h // 8, e // 128, 8, 128).transpose(0, 2, 1, 3)
    return out.reshape(2, h, e)


def solution(mesh):
    fine = Mesh(mesh.devices.reshape(8, 2, 2, 4, 2), ("z", "xh", "xl", "y", "c"))
    dp = ("xl", "y", "c")
    return jax.shard_map(
        local,
        mesh=fine,
        in_specs=(
            P(GROUP, dp, None),
            P(GROUP, dp, None),
            P(GROUP, None, dp, None),
            P(GROUP, None, dp, None),
            P(),
        ),
        out_specs=P(None, dp, None),
        check_vma=False,
    )
```

```python
import jax
import jax.numpy as jnp
from jax import lax
from jax.sharding import Mesh, PartitionSpec as P

BF = jnp.bfloat16
F32 = jnp.float32
CHIPS = ("xl", "y")
GROUP = ("z", "xh")


def shift_y(x, by):
    return lax.ppermute(x, "y", [(i, (i + by) % 4) for i in range(4)])


def swap_x(x):
    return lax.ppermute(x, "xl", [(0, 1), (1, 0)])


def swap_core(x):
    return lax.ppermute(x, "c", [(0, 1), (1, 0)])


def exchange(x, axes):
    return lax.all_to_all(x, axes, split_axis=0, concat_axis=0, tiled=True)


def dot(a, b, dims):
    return lax.dot_general(a, b, (dims, ((), ())), preferred_element_type=F32)


def embed(x, w):
    u = dot(x, w, ((1,), (0,)))
    nrm = jnp.sqrt(jnp.sum(u * u, axis=1, keepdims=True) + 1e-06)
    return u / nrm, nrm


def back_norm(unit, nrm, dz):
    return ((dz - unit * jnp.sum(unit * dz, axis=1, keepdims=True)) / nrm).astype(BF)


def after(x, *done):
    return lax.optimization_barrier((x, *done))[0]


def natural(held):
    both = jnp.stack([held, swap_core(held)], 2)
    y, xl, core = (lax.axis_index(name) for name in ("y", "xl", "c"))
    both = lax.dynamic_slice_in_dim(jnp.concatenate([both, both], 0), lax.rem(4 - y, 4), 4, 0)
    both = jnp.where(xl == 0, both, both[:, ::-1])
    both = jnp.where(core == 0, both, both[:, :, ::-1])
    return both.transpose(1, 0, 2, 3, 4).reshape(-1, held.shape[-1])


def gather_inputs(a, b, x_img, x_txt):
    cut = 40
    other = swap_x(a)
    pair = jnp.stack([a, other])
    below, above = shift_y(b, 1), shift_y(b, 3)
    a_below, a_above = shift_y(pair, 1), shift_y(pair, 3)
    near = jnp.stack([b, above, below])
    near_x = swap_x(near)
    far = jnp.concatenate([shift_y(below[:cut], 1), shift_y(above[cut:], 3)], 0)
    a_far = jnp.stack([shift_y(a_below[0], 1), shift_y(a_above[1], 3)])
    far_x = swap_x(far)
    held = [jnp.stack([near[0], near_x[0]]), jnp.stack([near[1], near_x[1]]), jnp.stack([far, far_x]), jnp.stack([near[2], near_x[2]])]
    w_b = natural(jnp.stack(held))
    w_a = natural(jnp.stack([pair, a_above, a_far, a_below]))
    x_img, x_txt = after(x_img, a_below, a_above), after(x_txt, a_below, a_above, far)
    return w_a, w_b, x_img, x_txt


def local(img_feat, txt_feat, group_weights, drift, logit_params):
    core = lax.axis_index("c")
    x_img, x_txt = img_feat[0], txt_feat[0]
    rows = x_img.shape[0]
    scale = jnp.exp(logit_params[0])
    bias = logit_params[1]

    w_img, w_txt, x_img, x_late = gather_inputs(group_weights[0, 0], group_weights[0, 1], x_img, x_txt)
    x_txt = x_late
    txt_x = swap_x(x_txt)
    below, above = shift_y(x_img, 1), shift_y(x_img, 3)
    half = rows // 2
    far = shift_y(below[:half], 1), shift_y(above[half:], 3)
    x_half = jnp.concatenate([x_txt, txt_x], 0)
    x_txt = jnp.concatenate([x_half, after(swap_core(x_half), w_txt, w_img)], 0)
    w_txt, x_txt = lax.optimization_barrier((w_txt, x_txt))
    zf_txt, n_txt = embed(x_txt, w_txt)
    *far, w_img = lax.optimization_barrier((*far, w_img, n_txt))[:3]
    x_img = jnp.concatenate([x_img, below, above, *far], 0)

    xl, y = lax.axis_index("xl"), lax.axis_index("y")
    at = lambda v, k, axis: lax.dynamic_index_in_dim(v, k, axis, keepdims=False)

    def columns(x):
        parts = x.T.reshape(2, 4, 2, -1, x.shape[0])
        parts = jnp.concatenate([parts, parts], 1)
        parts = lax.dynamic_slice_in_dim(parts, y, 4, 1)
        parts = jnp.stack([at(parts, xl, 0), at(parts, 1 - xl, 0)])
        pick = lambda k: at(parts, k, 2).reshape(-1, x.shape[0])
        return pick(core), pick(1 - core)

    keep_img, give_img = columns(x_img)
    keep_txt, _ = columns(x_txt)

    zf_img, n_img = embed(x_img, w_img)
    z_img, z_txt = zf_img.astype(BF), zf_txt.astype(BF)
    score = scale * dot(z_img, z_txt, ((1,), (1,))) + bias
    i = lax.broadcasted_iota(jnp.int32, score.shape, 0)
    j = lax.broadcasted_iota(jnp.int32, score.shape, 1)
    label = jnp.where((i == j) & (i < rows), 1.0, -1.0).astype(F32)
    gb = (-label * jax.nn.sigmoid(-label * score)).astype(BF)
    nn = ((1,), (0,))
    du_txt = back_norm(zf_txt, n_txt, scale * dot(gb, z_img, ((0,), (0,))))
    got_txt = swap_core(jnp.concatenate([du_txt[2 * rows :], du_txt[: 2 * rows]], 0))
    du_img = back_norm(zf_img, n_img, scale * dot(gb, z_txt, nn))
    got_img = swap_core(dot(give_img, du_img, nn).astype(BF))
    g_txt = dot(keep_txt, (du_txt.astype(F32) + got_txt.astype(F32)).astype(BF), nn).astype(BF)
    g_txt, got_img = lax.optimization_barrier((g_txt, got_img))
    g_img = dot(keep_img, du_img, nn)
    d, e = g_img.shape
    h = d // 8
    g_txt = g_txt.reshape(2, 4, h, e)
    g_img = (g_img + got_img.astype(F32)).astype(BF).reshape(2, 4, h, e)
    sums = lambda v: sum([v[0].astype(F32)] + [shift_y(v[k], k).astype(F32) for k in (1, 2, 3)])
    g_txt = sums(jnp.moveaxis(g_txt, 1, 0)).astype(BF)
    g_img = (g_img[0].astype(F32) + swap_x(g_img[1]).astype(F32)).astype(BF)
    g_txt = g_txt[0].astype(F32) + swap_x(g_txt[1]).astype(F32)
    g_img = sums(g_img)
    block = jnp.stack([g_img, g_txt]) + drift[0].astype(F32)
    tiles = block.reshape(2 * h // 8, 8, e // 128, 128).transpose(0, 2, 1, 3).reshape(-1, 8, 128)
    n = tiles.shape[0]
    each = -(-n // 16)
    tiles = jnp.pad(tiles, ((0, 16 * each - n), (0, 0), (0, 0))).reshape(16, each * 8, 128)
    total = jnp.sum(exchange(tiles.astype(BF), GROUP).astype(F32), axis=0) * (1.0 / 16)
    out = exchange(jnp.broadcast_to(total.astype(BF)[None], (16, each * 8, 128)), GROUP).astype(F32)
    out = out.reshape(16 * each, 8, 128)[:n].reshape(2 * h // 8, e // 128, 8, 128).transpose(0, 2, 1, 3)
    return out.reshape(2, h, e)


def solution(mesh):
    fine = Mesh(mesh.devices.reshape(8, 2, 2, 4, 2), ("z", "xh", "xl", "y", "c"))
    dp = ("xl", "y", "c")
    return jax.shard_map(
        local,
        mesh=fine,
        in_specs=(
            P(GROUP, dp, None),
            P(GROUP, dp, None),
            P(GROUP, None, dp, None),
            P(GROUP, None, dp, None),
            P(),
        ),
        out_specs=P(None, dp, None),
        check_vma=False,
    )
```

```python
import jax
import jax.numpy as jnp
from jax import lax
from jax.sharding import Mesh, PartitionSpec as P

BF = jnp.bfloat16
F32 = jnp.float32
CHIPS = ("xl", "y")
GROUP = ("z", "xh")


def shift_y(x, by):
    return lax.ppermute(x, "y", [(i, (i + by) % 4) for i in range(4)])


def swap_x(x):
    return lax.ppermute(x, "xl", [(0, 1), (1, 0)])


def swap_core(x):
    return lax.ppermute(x, "c", [(0, 1), (1, 0)])


def exchange(x, axes):
    return lax.all_to_all(x, axes, split_axis=0, concat_axis=0, tiled=True)


def dot(a, b, dims):
    return lax.dot_general(a, b, (dims, ((), ())), preferred_element_type=F32)


def embed(x, w):
    u = dot(x, w, ((1,), (0,)))
    inv = lax.rsqrt(jnp.sum(u * u, axis=1, keepdims=True) + 1e-06)
    return u * inv, inv


def back_norm(unit, inv, dz):
    return ((dz - unit * jnp.sum(unit * dz, axis=1, keepdims=True)) * inv).astype(BF)


def after(x, *done):
    return lax.optimization_barrier((x, *done))[0]


def natural(held):
    both = jnp.stack([held, swap_core(held)], 2)
    y, xl, core = (lax.axis_index(name) for name in ("y", "xl", "c"))
    both = lax.dynamic_slice_in_dim(jnp.concatenate([both, both], 0), lax.rem(4 - y, 4), 4, 0)
    both = jnp.where(xl == 0, both, both[:, ::-1])
    both = jnp.where(core == 0, both, both[:, :, ::-1])
    return both.transpose(1, 0, 2, 3, 4).reshape(-1, held.shape[-1])


def gather_inputs(a, b, x_img, x_txt):
    cut = 40
    other = swap_x(a)
    pair = jnp.stack([a, other])
    below, above = shift_y(b, 1), shift_y(b, 3)
    a_below, a_above = shift_y(pair, 1), shift_y(pair, 3)
    near = jnp.stack([b, above, below])
    near_x = swap_x(near)
    far = jnp.concatenate([shift_y(below[:cut], 1), shift_y(above[cut:], 3)], 0)
    a_far = jnp.stack([shift_y(a_below[0], 1), shift_y(a_above[1], 3)])
    far_x = swap_x(far)
    held = [jnp.stack([near[0], near_x[0]]), jnp.stack([near[1], near_x[1]]), jnp.stack([far, far_x]), jnp.stack([near[2], near_x[2]])]
    w_b = natural(jnp.stack(held))
    w_a = natural(jnp.stack([pair, a_above, a_far, a_below]))
    x_img, x_txt = after(x_img, a_below, a_above), after(x_txt, a_below, a_above, far)
    return w_a, w_b, x_img, x_txt


def local(img_feat, txt_feat, group_weights, drift, logit_params):
    core = lax.axis_index("c")
    x_img, x_txt = img_feat[0], txt_feat[0]
    rows = x_img.shape[0]
    scale = jnp.exp(logit_params[0])
    bias = logit_params[1]

    w_img, w_txt, x_img, x_late = gather_inputs(group_weights[0, 0], group_weights[0, 1], x_img, x_txt)
    x_txt = x_late
    txt_x = swap_x(x_txt)
    below, above = shift_y(x_img, 1), shift_y(x_img, 3)
    half = rows // 2
    far = shift_y(below[:half], 1), shift_y(above[half:], 3)
    x_half = jnp.concatenate([x_txt, txt_x], 0)
    x_txt = jnp.concatenate([x_half, after(swap_core(x_half), w_txt, w_img)], 0)
    w_txt, x_txt = lax.optimization_barrier((w_txt, x_txt))
    zf_txt, n_txt = embed(x_txt, w_txt)
    *far, w_img = lax.optimization_barrier((*far, w_img, n_txt))[:3]
    x_img = jnp.concatenate([x_img, below, above, *far], 0)

    xl, y = lax.axis_index("xl"), lax.axis_index("y")
    at = lambda v, k, axis: lax.dynamic_index_in_dim(v, k, axis, keepdims=False)

    def columns(x):
        parts = x.T.reshape(2, 4, 2, -1, x.shape[0])
        parts = jnp.concatenate([parts, parts], 1)
        parts = lax.dynamic_slice_in_dim(parts, y, 4, 1)
        parts = jnp.stack([at(parts, xl, 0), at(parts, 1 - xl, 0)])
        pick = lambda k: at(parts, k, 2).reshape(-1, x.shape[0])
        return pick(core), pick(1 - core)

    keep_img, give_img = columns(x_img)
    keep_txt, _ = columns(x_txt)

    zf_img, n_img = embed(x_img, w_img)
    z_img, z_txt = zf_img.astype(BF), zf_txt.astype(BF)
    score = scale * dot(z_img, z_txt, ((1,), (1,))) + bias
    i = lax.broadcasted_iota(jnp.int32, score.shape, 0)
    j = lax.broadcasted_iota(jnp.int32, score.shape, 1)
    label = jnp.where((i == j) & (i < rows), 1.0, -1.0).astype(F32)
    gb = (-label * jax.nn.sigmoid(-label * score)).astype(BF)
    nn = ((1,), (0,))
    du_txt = back_norm(zf_txt, n_txt, scale * dot(gb, z_img, ((0,), (0,))))
    got_txt = swap_core(jnp.concatenate([du_txt[2 * rows :], du_txt[: 2 * rows]], 0))
    du_img = back_norm(zf_img, n_img, scale * dot(gb, z_txt, nn))
    got_img = swap_core(dot(give_img, du_img, nn).astype(BF))
    g_txt = dot(keep_txt, (du_txt.astype(F32) + got_txt.astype(F32)).astype(BF), nn).astype(BF)
    g_txt, got_img = lax.optimization_barrier((g_txt, got_img))
    g_img = dot(keep_img, du_img, nn)
    d, e = g_img.shape
    h = d // 8
    g_txt = g_txt.reshape(2, 4, h, e)
    g_img = (g_img + got_img.astype(F32)).astype(BF).reshape(2, 4, h, e)
    sums = lambda v: sum([v[0].astype(F32)] + [shift_y(v[k], k).astype(F32) for k in (1, 2, 3)])
    g_txt = sums(jnp.moveaxis(g_txt, 1, 0)).astype(BF)
    g_img = (g_img[0].astype(F32) + swap_x(g_img[1]).astype(F32)).astype(BF)
    g_txt = g_txt[0].astype(F32) + swap_x(g_txt[1]).astype(F32)
    g_img = sums(g_img)
    block = jnp.stack([g_img, g_txt]) + drift[0].astype(F32)
    tiles = block.reshape(2 * h // 8, 8, e // 128, 128).transpose(0, 2, 1, 3).reshape(-1, 8, 128)
    n = tiles.shape[0]
    each = -(-n // 16)
    tiles = jnp.pad(tiles, ((0, 16 * each - n), (0, 0), (0, 0))).reshape(16, each * 8, 128)
    total = jnp.sum(exchange(tiles.astype(BF), GROUP).astype(F32), axis=0) * (1.0 / 16)
    out = exchange(jnp.broadcast_to(total.astype(BF)[None], (16, each * 8, 128)), GROUP).astype(F32)
    out = out.reshape(16 * each, 8, 128)[:n].reshape(2 * h // 8, e // 128, 8, 128).transpose(0, 2, 1, 3)
    return out.reshape(2, h, e)


def solution(mesh):
    fine = Mesh(mesh.devices.reshape(8, 2, 2, 4, 2), ("z", "xh", "xl", "y", "c"))
    dp = ("xl", "y", "c")
    return jax.shard_map(
        local,
        mesh=fine,
        in_specs=(
            P(GROUP, dp, None),
            P(GROUP, dp, None),
            P(GROUP, None, dp, None),
            P(GROUP, None, dp, None),
            P(),
        ),
        out_specs=P(None, dp, None),
        check_vma=False,
    )
```

```python
import jax
import jax.numpy as jnp
from jax import lax
from jax.sharding import Mesh, PartitionSpec as P

BF = jnp.bfloat16
F32 = jnp.float32
CHIPS = ("xl", "y")
GROUP = ("z", "xh")


def shift_y(x, by):
    return lax.ppermute(x, "y", [(i, (i + by) % 4) for i in range(4)])


def swap_x(x):
    return lax.ppermute(x, "xl", [(0, 1), (1, 0)])


def swap_core(x):
    return lax.ppermute(x, "c", [(0, 1), (1, 0)])


def exchange(x, axes):
    return lax.all_to_all(x, axes, split_axis=0, concat_axis=0, tiled=True)


def dot(a, b, dims):
    return lax.dot_general(a, b, (dims, ((), ())), preferred_element_type=F32)


def embed(x, w):
    u = dot(x, w, ((1,), (0,)))
    nrm = jnp.sqrt(jnp.sum(u * u, axis=1, keepdims=True) + 1e-06)
    return u / nrm, nrm


def back_norm(unit, nrm, dz):
    return ((dz - unit * jnp.sum(unit * dz, axis=1, keepdims=True)) / nrm).astype(BF)


def after(x, *done):
    return lax.optimization_barrier((x, *done))[0]


def natural(held):
    both = jnp.stack([held, swap_core(held)], 2)
    y, xl, core = (lax.axis_index(name) for name in ("y", "xl", "c"))
    both = lax.dynamic_slice_in_dim(jnp.concatenate([both, both], 0), lax.rem(4 - y, 4), 4, 0)
    both = jnp.where(xl == 0, both, both[:, ::-1])
    both = jnp.where(core == 0, both, both[:, :, ::-1])
    return both.transpose(1, 0, 2, 3, 4).reshape(-1, held.shape[-1])


def placed(held):
    y, xl, core = (lax.axis_index(name) for name in ("y", "xl", "c"))
    out = jnp.zeros((16, *held.shape[2:]), held.dtype)
    for source, c in ((held, core), (swap_core(held), 1 - core)):
        for k in range(4):
            for x in range(2):
                at = (lax.rem(xl + x, 2) * 4 + lax.rem(y + k, 4)) * 2 + c
                out = lax.dynamic_update_index_in_dim(out, source[k, x], at, 0)
    return out.reshape(-1, held.shape[-1])


def gather_inputs(a, b, x_img, x_txt):
    cut = 40
    other = swap_x(a)
    pair = jnp.stack([a, other])
    below, above = shift_y(b, 1), shift_y(b, 3)
    a_below, a_above = shift_y(pair, 1), shift_y(pair, 3)
    near = jnp.stack([b, above, below])
    near_x = swap_x(near)
    far = jnp.concatenate([shift_y(below[:cut], 1), shift_y(above[cut:], 3)], 0)
    a_far = jnp.stack([shift_y(a_below[0], 1), shift_y(a_above[1], 3)])
    far_x = swap_x(far)
    held = [jnp.stack([near[0], near_x[0]]), jnp.stack([near[1], near_x[1]]), jnp.stack([far, far_x]), jnp.stack([near[2], near_x[2]])]
    w_b = placed(jnp.stack(held))
    w_a = natural(jnp.stack([pair, a_above, a_far, a_below]))
    x_img, x_txt = after(x_img, a_below, a_above), after(x_txt, a_below, a_above, far)
    return w_a, w_b, x_img, x_txt


def local(img_feat, txt_feat, group_weights, drift, logit_params):
    core = lax.axis_index("c")
    x_img, x_txt = img_feat[0], txt_feat[0]
    rows = x_img.shape[0]
    scale = jnp.exp(logit_params[0])
    bias = logit_params[1]

    w_img, w_txt, x_img, x_late = gather_inputs(group_weights[0, 0], group_weights[0, 1], x_img, x_txt)
    x_txt = x_late
    txt_x = swap_x(x_txt)
    below, above = shift_y(x_img, 1), shift_y(x_img, 3)
    half = rows // 2
    far = shift_y(below[:half], 1), shift_y(above[half:], 3)
    x_half = jnp.concatenate([x_txt, txt_x], 0)
    x_txt = jnp.concatenate([x_half, after(swap_core(x_half), w_txt, w_img)], 0)
    w_txt, x_txt = lax.optimization_barrier((w_txt, x_txt))
    zf_txt, n_txt = embed(x_txt, w_txt)
    *far, w_img = lax.optimization_barrier((*far, w_img, n_txt))[:3]
    x_img = jnp.concatenate([x_img, below, above, *far], 0)

    xl, y = lax.axis_index("xl"), lax.axis_index("y")
    at = lambda v, k, axis: lax.dynamic_index_in_dim(v, k, axis, keepdims=False)

    def columns(x):
        parts = x.T.reshape(2, 4, 2, -1, x.shape[0])
        parts = jnp.concatenate([parts, parts], 1)
        parts = lax.dynamic_slice_in_dim(parts, y, 4, 1)
        parts = jnp.stack([at(parts, xl, 0), at(parts, 1 - xl, 0)])
        pick = lambda k: at(parts, k, 2).reshape(-1, x.shape[0])
        return pick(core), pick(1 - core)

    keep_img, give_img = columns(x_img)
    keep_txt, _ = columns(x_txt)

    zf_img, n_img = embed(x_img, w_img)
    z_img, z_txt = zf_img.astype(BF), zf_txt.astype(BF)
    score = scale * dot(z_img, z_txt, ((1,), (1,))) + bias
    i = lax.broadcasted_iota(jnp.int32, score.shape, 0)
    j = lax.broadcasted_iota(jnp.int32, score.shape, 1)
    label = jnp.where((i == j) & (i < rows), 1.0, -1.0).astype(F32)
    gb = (-label * jax.nn.sigmoid(-label * score)).astype(BF)
    nn = ((1,), (0,))
    du_txt = back_norm(zf_txt, n_txt, scale * dot(gb, z_img, ((0,), (0,))))
    got_txt = swap_core(jnp.concatenate([du_txt[2 * rows :], du_txt[: 2 * rows]], 0))
    du_img = back_norm(zf_img, n_img, scale * dot(gb, z_txt, nn))
    got_img = swap_core(dot(give_img, du_img, nn).astype(BF))
    g_txt = dot(keep_txt, (du_txt.astype(F32) + got_txt.astype(F32)).astype(BF), nn).astype(BF)
    g_txt, got_img = lax.optimization_barrier((g_txt, got_img))
    g_img = dot(keep_img, du_img, nn)
    d, e = g_img.shape
    h = d // 8
    g_txt = g_txt.reshape(2, 4, h, e)
    g_img = (g_img + got_img.astype(F32)).astype(BF).reshape(2, 4, h, e)
    sums = lambda v: sum([v[0].astype(F32)] + [shift_y(v[k], k).astype(F32) for k in (1, 2, 3)])
    g_txt = sums(jnp.moveaxis(g_txt, 1, 0)).astype(BF)
    g_img = (g_img[0].astype(F32) + swap_x(g_img[1]).astype(F32)).astype(BF)
    g_txt = g_txt[0].astype(F32) + swap_x(g_txt[1]).astype(F32)
    g_img = sums(g_img)
    block = jnp.stack([g_img, g_txt]) + drift[0].astype(F32)
    tiles = block.reshape(2 * h // 8, 8, e // 128, 128).transpose(0, 2, 1, 3).reshape(-1, 8, 128)
    n = tiles.shape[0]
    each = -(-n // 16)
    tiles = jnp.pad(tiles, ((0, 16 * each - n), (0, 0), (0, 0))).reshape(16, each * 8, 128)
    total = jnp.sum(exchange(tiles.astype(BF), GROUP).astype(F32), axis=0) * (1.0 / 16)
    out = exchange(jnp.broadcast_to(total.astype(BF)[None], (16, each * 8, 128)), GROUP).astype(F32)
    out = out.reshape(16 * each, 8, 128)[:n].reshape(2 * h // 8, e // 128, 8, 128).transpose(0, 2, 1, 3)
    return out.reshape(2, h, e)


def solution(mesh):
    fine = Mesh(mesh.devices.reshape(8, 2, 2, 4, 2), ("z", "xh", "xl", "y", "c"))
    dp = ("xl", "y", "c")
    return jax.shard_map(
        local,
        mesh=fine,
        in_specs=(
            P(GROUP, dp, None),
            P(GROUP, dp, None),
            P(GROUP, None, dp, None),
            P(GROUP, None, dp, None),
            P(),
        ),
        out_specs=P(None, dp, None),
        check_vma=False,
    )
```
